32 devices in a mesh: row: 8 (over z, y), col: 4 (over x, core).
Axes of the slice: x: 2, y: 2, z: 4, core: 2. Of those that a mesh axis runs over, the one named last changes fastest.
Arguments:
- kernel_panel: float32 [4096, 512], P('row', 'col'), may hold values from -66 to 66, as said below
- kernel_slab: float32 [4096, 2048], P('row', 'col'), may hold values from -6 to 6
Outputs:
- factor_panel: float32 [4096, 512], P('row', 'col')
- schur_slab: float32 [4096, 2048], P('row', 'col')
The draws below stay inside these ranges and needn't reach their ends.
Inputs may be any that keep to these rules, and one draw needn't show every extreme that they name: `kernel_panel`: the first 512 rows form a symmetric positive definite matrix whose smallest eigenvalue is 0.5 or more.
All inputs are finite; a program needn't handle non-finite values.
Results may differ from the reference program's by a relative error of at most 0.00011.
Values sent between devices are 32-bit elements; how exact they have to be, the bound alone decides.
A program may use at most 64 MiB of HBM per device.

```python
import jax
import jax.numpy as jnp
from jax import lax

PANEL = 512
ROWS_DEV = 512
ORDER = 4096
SLAB = 2048
N_ROW = 8


def draw_kernel_panel(key, part):
    key_gram = jax.random.fold_in(key, 11)
    key_rest = jax.random.fold_in(key, 12)
    source = jax.random.truncated_normal(key_gram, -4.0, 4.0, (PANEL, PANEL), jnp.float32)
    gram = jnp.dot(source, source.T, precision=lax.Precision.HIGHEST) / PANEL
    leading_block = 0.5 * (gram + gram.T) + 0.5 * jnp.eye(PANEL, dtype=jnp.float32)
    rest_rows = 0.25 * jax.random.truncated_normal(key_rest, -4.0, 4.0, (ORDER - PANEL, PANEL), jnp.float32)
    return jnp.concatenate([leading_block, rest_rows], axis=0)


def block_levels(stream_key, dims, shards, smallest, high):
    gain = 1.0
    for dim, blocks in shards:
        steps = jax.random.uniform(jax.random.fold_in(jax.random.fold_in(stream_key, 6), dim), (blocks,), jnp.float32, smallest / len(shards), high / len(shards))
        gain = gain * jnp.repeat(jnp.exp(steps), dims[dim] // blocks).reshape((-1,) + (1,) * (len(dims) - 1 - dim))
    return gain


def centred(rng, dims, width, reach, pieces=(), kind=jnp.bfloat16):
    values = width * jax.random.normal(rng, dims, jnp.float32)
    if pieces:
        values = values * block_levels(rng, dims, pieces, -0.22, 0.18)
    return jnp.clip(values, -reach, reach).astype(kind)


def setup_inputs(seed: int = 0) -> dict:
    keys = jax.random.split(jax.random.key(seed), 3)
    return {
        "kernel_panel": draw_kernel_panel(jax.random.fold_in(keys[2], 71), 0),
        "kernel_slab": centred(keys[1], (ORDER, SLAB), 1.0, 6.0, ((0, 8), (1, 4)), jnp.float32),
    }


def reference(kernel_panel, kernel_slab):
    leading_block = kernel_panel[:PANEL]
    leading_factor = jnp.linalg.cholesky(leading_block)
    lower_full = jax.scipy.linalg.solve_triangular(leading_factor, kernel_panel.T, lower=True).T
    row_ids = lax.iota(jnp.int32, ORDER)
    col_ids = lax.iota(jnp.int32, PANEL)
    lower_full = jnp.where(col_ids[None, :] <= row_ids[:, None], lower_full, jnp.zeros_like(lower_full))
    block_ids = lax.iota(jnp.int32, SLAB // ROWS_DEV)
    row_table = ((1 + block_ids % (N_ROW - 1)) * ROWS_DEV)[:, None] + lax.iota(jnp.int32, ROWS_DEV)[None, :]
    far_rows = jnp.take(lower_full, row_table.reshape(-1).astype(jnp.int32), axis=0)
    update = lax.dot_general(lower_full.astype(jnp.float32), far_rows.astype(jnp.float32), (((1,), (1,)), ((), ())), precision=lax.Precision.HIGHEST, preferred_element_type=jnp.float32)
    return (lower_full, kernel_slab - update)
```

```python
import functools

import jax
import jax.numpy as jnp
from jax import lax
from jax.experimental import pallas as pl
from jax.experimental.pallas import tpu as pltpu
from jax.sharding import PartitionSpec as P

F32, BF16 = jnp.float32, jnp.bfloat16
SUB = 8
MID = 32


def split(x):
    high = x.astype(BF16)
    return high, (x - high.astype(F32)).astype(BF16)


def dot(a, b, dims):
    return lax.dot_general(a, b, (dims, ((), ())), preferred_element_type=F32)


def dot3(a, b, dims=((1,), (1,))):
    (ah, al), (bh, bl) = a, b
    return dot(ah, bh, dims) + (dot(ah, bl, dims) + dot(al, bh, dims))


def sublane(x, j):
    return jnp.broadcast_to(x[j : j + 1, :], x.shape)


def lane(x, j):
    return jnp.broadcast_to(x[:, j : j + 1], x.shape)


def newton_reciprocal(d):
    r = pl.reciprocal(d, approx=True)
    r = r * (2.0 - d * r)
    return r * (2.0 - d * r)


def lower_inverse(square, hook):
    n = square.shape[0]
    count = n // SUB
    row_ids = lax.broadcasted_iota(jnp.int32, (SUB, n), 0)
    lane_ids = lax.broadcasted_iota(jnp.int32, (SUB, n), 1)
    work = [square[SUB * i : SUB * (i + 1)] for i in range(count)]
    unit = [jnp.where(lane_ids == row_ids + SUB * i, 1.0, 0.0).astype(F32) for i in range(count)]
    per = MID // SUB
    for b in range(n // MID):
        last = per * (b + 1)
        for t in range(per * b, last):
            cols = {i: [lane(work[i], SUB * t + j) for j in range(SUB)] for i in range(t, last)}
            pivots = jnp.ones((SUB, n), F32)
            for j in range(SUB):
                pivot = sublane(cols[t][j], j)
                inverse = newton_reciprocal(pivot)
                pivots = jnp.where(row_ids == j, pivot, pivots)
                work_row, unit_row = sublane(work[t], j), sublane(unit[t], j)
                heads = {k: sublane(cols[t][k], j) for k in range(j + 1, SUB)}
                for i in range(t, last):
                    column = cols[i][j]
                    if i == t:
                        column = jnp.where(row_ids > j, column, 0.0)
                    factor = column * inverse
                    for k in range(j + 1, SUB):
                        cols[i][k] = cols[i][k] - factor * heads[k]
                    work[i] = work[i] - factor * work_row
                    unit[i] = unit[i] - factor * unit_row
            scale = lax.rsqrt(pivots)
            scale = scale * (1.5 - 0.5 * pivots * scale * scale)
            work[t] = work[t] * scale
            unit[t] = unit[t] * scale
        if last < count:
            rows = jnp.concatenate(work[per * b : last], axis=0)
            both = jnp.concatenate([rows, jnp.concatenate(unit[per * b : last], axis=0)], axis=1)
            rh, rl = split(rows)
            bh, bl = split(both)
            left = jnp.concatenate([rh, rh, rl], axis=0)
            right = jnp.concatenate([bh, bl, bh], axis=0)
            update = dot(left, right, ((0,), (0,)))
            for i in range(last, count):
                work[i] = work[i] - update[SUB * i : SUB * (i + 1), :n]
                unit[i] = unit[i] - update[SUB * i : SUB * (i + 1), n:]
        hook()
    return jnp.concatenate(unit, axis=0)


def kernel(rows_count, cols_count, panel, slab, factor_out, schur_out,
           lead, rows, far, low_h, low_l, own_h, own_l, far_h, far_l,
           lead_recv, rows_recv, far_recv, lead_down, lead_cross, lead_sib, lead_par,
           rows_sib, rows_par, far_up, far_down, far_cross):
    r, c = lax.axis_index("row"), lax.axis_index("col")
    size, width = panel.shape
    chunks = cols_count
    step = size // chunks
    core = c % 2
    sibling = c + 1 - 2 * core
    partner = r + 1 - 2 * (r % 2)
    pairs = cols_count // 2
    root = 1 + c % (rows_count - 1)
    on_chain = (root % 2) == (r % 2)

    def to(row, col):
        return {"row": row, "col": col}

    def peer(i):
        return 2 * ((c // 2 + i + 1) % pairs) + core

    barrier = pltpu.get_barrier_semaphore()

    def greet(row, col):
        pl.semaphore_signal(barrier, inc=1, device_id=to(row, col), device_id_type=pl.DeviceIdType.MESH)

    greet(r, sibling)
    for i in range(pairs - 1):
        greet(r, peer(i))
    greet(partner, c)
    has_up, has_down = r >= 2, r + 2 < rows_count

    @pl.when(has_up)
    def _():
        greet(r - 2, c)

    @pl.when(has_down)
    def _():
        greet(r + 2, c)

    rows[c] = panel[...]

    @pl.when(r == 0)
    def _():
        lead[c] = panel[...]

    pl.semaphore_wait(barrier, 1 + pairs + has_up.astype(jnp.int32) + has_down.astype(jnp.int32))

    def copy(src, dst, send, recv, row, col):
        return pltpu.make_async_remote_copy(src_ref=src, dst_ref=dst, send_sem=send, recv_sem=recv,
                                            device_id=to(row, col), device_id_type=pl.DeviceIdType.MESH)

    def lead_copy(block, q, send, row, col):
        part = lead.at[block, pl.ds(q * step, step), :]
        return copy(part, part, send, lead_recv.at[block, q], row, col)

    def rows_copy(block, send, col):
        return copy(rows.at[block], rows.at[block], send, rows_recv.at[block], r, col)

    def far_copy(block, send, row):
        return copy(far.at[block], far.at[block], send, far_recv.at[block], row, c)

    def lead_arrived(block, q):
        lead_copy(block, q, lead_down.at[0], r, sibling).wait_recv()

    def rows_arrived(block):
        rows_copy(block, rows_par.at[0], sibling).wait_recv()

    def far_arrived(block):
        far_copy(block, far_up.at[0], partner).wait_recv()

    for q in range(chunks):
        @pl.when(r > 0)
        def _():
            lead_arrived(c, q)

        @pl.when(has_down)
        def _():
            lead_copy(c, q, lead_down.at[q], r + 2, c).start()

        @pl.when(r == 0)
        def _():
            lead_copy(c, q, lead_cross.at[q], 1, c).start()

        for i in range(pairs - 1):
            lead_copy(c, q, lead_par.at[i, q], r, peer(i)).start()
        lead_copy(c, q, lead_sib.at[0, q], r, sibling).start()
    for i in range(pairs - 1):
        rows_copy(c, rows_par.at[i], peer(i)).start()
    rows_copy(c, rows_sib.at[0], sibling).start()
    for q in range(chunks):
        for i in range(pairs - 1):
            lead_arrived(peer(i), q)
            lead_copy(peer(i), q, lead_sib.at[i + 1, q], r, sibling).start()

    def rows_ready(block):
        @pl.when(block % 2 != core)
        def _():
            rows_arrived(block)

    reach = (rows_count + 1) // 2
    distance = jnp.abs(root - r) // 2
    hooks = cols_count + reach
    state = {"point": 0, "next": 0}

    def forward(m):
        q = m - distance

        @pl.when(on_chain & (q >= 0) & (q < cols_count))
        def _():
            @pl.when(r == root)
            def _():
                @pl.when(q % 2 != core)
                def _():
                    rows_arrived(q)

                far[q] = rows[q]

            @pl.when(r != root)
            def _():
                far_arrived(q)

            @pl.when((r <= root) & has_up)
            def _():
                far_copy(q, far_up.at[q], r - 2).start()

            @pl.when((r >= root) & has_down)
            def _():
                far_copy(q, far_down.at[q], r + 2).start()

            far_copy(q, far_cross.at[q], partner).start()

    def hook():
        state["point"] += 1
        if state["point"] == 1:
            for i in range(pairs - 1):
                rows_arrived(peer(i))
                rows_copy(peer(i), rows_sib.at[i + 1], sibling).start()
        elif state["point"] % 2 == 0 and state["next"] < hooks:
            forward(state["next"])
            state["next"] += 1

    lane_ids = lax.broadcasted_iota(jnp.int32, (size, width), 1)
    row_ids = lax.broadcasted_iota(jnp.int32, (size, width), 0)

    def solve(block, k, source, high, low, inverse, top):
        done = k * width
        value = source[k, top:, :]
        if k:
            value = value - dot3((high[top:, :done], low[top:, :done]),
                                 (low_h[done : done + width, :done], low_l[done : done + width, :done]))
        return dot3(split(value), inverse)

    def keep(x, k, high, low, top):
        xh, xl = split(x)
        high[top:, k * width : (k + 1) * width] = xh
        low[top:, k * width : (k + 1) * width] = xl

    inverses = []
    for k in range(cols_count):
        @pl.when(k % 2 != core)
        def _():
            for q in range(chunks):
                lead_arrived(k, q)

        first, end = k * width, (k + 1) * width
        square = lead[k, first:end, :]
        if k:
            square = square - dot3((low_h[first:end, :first], low_l[first:end, :first]),
                                   (low_h[first:end, :first], low_l[first:end, :first]))
        inverse = split(lower_inverse(square, hook))
        inverses.append(inverse)
        if k + 1 < cols_count:
            keep(solve(None, k, lead, low_h, low_l, inverse, end), k, low_h, low_l, end)

    for k in range(cols_count):
        @pl.when((r != root) & (k % 2 != core))
        def _():
            rows_arrived(k)

        x = solve(None, k, rows, own_h, own_l, inverses[k], 0)
        x = jnp.where(k * width + lane_ids <= r * size + row_ids, x, 0.0)
        keep(x, k, own_h, own_l, 0)

        @pl.when(c == k)
        def _():
            factor_out[...] = x

    if state["next"] < hooks:
        def rest(m, carry):
            forward(m)
            return carry

        lax.fori_loop(state["next"], hooks, rest, 0)
    for k in range(cols_count):
        @pl.when(jnp.logical_not(on_chain))
        def _():
            far_arrived(k)

        x = solve(None, k, far, far_h, far_l, inverses[k], 0)
        x = jnp.where(k * width + lane_ids <= root * size + row_ids, x, 0.0)
        keep(x, k, far_h, far_l, 0)
    schur_out[...] = slab[...] - dot3((own_h[...], own_l[...]), (far_h[...], far_l[...]))

    for q in range(chunks):
        @pl.when(has_down)
        def _():
            lead_copy(c, q, lead_down.at[q], r + 2, c).wait_send()

        @pl.when(r == 0)
        def _():
            lead_copy(c, q, lead_cross.at[q], 1, c).wait_send()

        for i in range(pairs - 1):
            lead_copy(c, q, lead_par.at[i, q], r, peer(i)).wait_send()
            lead_copy(peer(i), q, lead_sib.at[i + 1, q], r, sibling).wait_send()
        lead_copy(c, q, lead_sib.at[0, q], r, sibling).wait_send()
    rows_copy(c, rows_sib.at[0], sibling).wait_send()
    for i in range(pairs - 1):
        rows_copy(c, rows_par.at[i], peer(i)).wait_send()
        rows_copy(peer(i), rows_sib.at[i + 1], sibling).wait_send()

    @pl.when(on_chain)
    def _():
        for q in range(cols_count):
            @pl.when((r <= root) & has_up)
            def _():
                far_copy(q, far_up.at[q], r - 2).wait_send()

            @pl.when((r >= root) & has_down)
            def _():
                far_copy(q, far_down.at[q], r + 2).wait_send()

            far_copy(q, far_cross.at[q], partner).wait_send()


def shards(rows_count, cols_count, panel, slab):
    size, width = panel.shape
    whole = cols_count * width
    pairs = cols_count // 2
    dma = pltpu.SemaphoreType.DMA
    block = pltpu.VMEM((cols_count, size, width), F32)
    half = pltpu.VMEM((size, whole), BF16)
    vmem = pl.BlockSpec(memory_space=pltpu.VMEM)
    return pl.pallas_call(
        functools.partial(kernel, rows_count, cols_count),
        out_shape=(jax.ShapeDtypeStruct(panel.shape, F32), jax.ShapeDtypeStruct(slab.shape, F32)),
        in_specs=[vmem, vmem],
        out_specs=(vmem, vmem),
        scratch_shapes=[
            block, block, block, half, half, half, half, half, half,
            dma((cols_count, cols_count)), dma((cols_count,)), dma((cols_count,)),
            dma((cols_count,)), dma((cols_count,)), dma((pairs, cols_count)), dma((pairs, cols_count)),
            dma((pairs,)), dma((pairs,)),
            dma((cols_count,)), dma((cols_count,)), dma((cols_count,)),
        ],
        compiler_params=pltpu.CompilerParams(
            collective_id=0, has_side_effects=True, vmem_limit_bytes=48 * 1024 * 1024
        ),
    )(panel, slab)


def solution(mesh):
    placed = (P("row", "col"), P("row", "col"))
    return jax.shard_map(
        functools.partial(shards, mesh.shape["row"], mesh.shape["col"]),
        mesh=mesh,
        in_specs=placed,
        out_specs=placed,
        check_vma=False,
    )
```

```python
import functools

import jax
import jax.numpy as jnp
from jax import lax
from jax.experimental import pallas as pl
from jax.experimental.pallas import tpu as pltpu
from jax.sharding import PartitionSpec as P

F32, BF16 = jnp.float32, jnp.bfloat16
SUB = 8
MID = 32


def split(x):
    high = x.astype(BF16)
    return high, (x - high.astype(F32)).astype(BF16)


def dot(a, b, dims):
    return lax.dot_general(a, b, (dims, ((), ())), preferred_element_type=F32)


def dot3(a, b, dims=((1,), (1,))):
    (ah, al), (bh, bl) = a, b
    return dot(ah, bh, dims) + (dot(ah, bl, dims) + dot(al, bh, dims))


def sublane(x, j):
    return jnp.broadcast_to(x[j : j + 1, :], x.shape)


def lane(x, j):
    return jnp.broadcast_to(x[:, j : j + 1], x.shape)


def inverse_root(p):
    s = lax.rsqrt(p)
    return s * (1.5 - 0.5 * p * s * s)


def lower_inverse(square, hook):
    n = square.shape[0]
    count = n // SUB
    row_ids = lax.broadcasted_iota(jnp.int32, (SUB, n), 0)
    lane_ids = lax.broadcasted_iota(jnp.int32, (SUB, n), 1)
    work = [square[SUB * i : SUB * (i + 1)] for i in range(count)]
    unit = [jnp.where(lane_ids == row_ids + SUB * i, 1.0, 0.0).astype(F32) for i in range(count)]
    per = MID // SUB
    for b in range(n // MID):
        last = per * (b + 1)
        for t in range(per * b, last):
            cols = {i: [lane(work[i], SUB * t + j) for j in range(SUB)] for i in range(t, last)}
            d1s = jnp.ones((SUB, n), F32); d2s = d1s; es = jnp.zeros((SUB, n), F32)
            for j in range(0, SUB, 2):
                top, nxt = cols[t][j], cols[t][j + 1]
                d1, e, d2 = sublane(top, j), sublane(nxt, j), sublane(nxt, j + 1)
                det = d1 * d2 - e * e
                inv = pl.reciprocal(det, approx=True)
                first, second = row_ids == j, row_ids == j + 1
                d1s = jnp.where(first | second, d1, d1s)
                es = jnp.where(second, e, es)
                d2s = jnp.where(second, d2, d2s)
                def mixed(x):
                    h1, h2 = sublane(x, j), sublane(x, j + 1)
                    return h1 * d2 - h2 * e, h2 * d1 - h1 * e
                heads = {k: mixed(cols[t][k]) for k in range(j + 2, SUB)}
                wg, ug = mixed(work[t]), mixed(unit[t])
                for i in range(t, last):
                    c1, c2 = cols[i][j], cols[i][j + 1]
                    if i == t:
                        below = row_ids > j + 1
                        c1, c2 = jnp.where(below, c1, 0.0), jnp.where(below, c2, 0.0)
                    for k in range(j + 2, SUB):
                        g1, g2 = heads[k]
                        cols[i][k] = cols[i][k] - (c1 * g1 + c2 * g2) * inv
                    work[i] = work[i] - (c1 * wg[0] + c2 * wg[1]) * inv
                    unit[i] = unit[i] - (c1 * ug[0] + c2 * ug[1]) * inv
            odd = row_ids % 2 == 1
            r1 = pl.reciprocal(d1s, approx=True)
            r1 = r1 * (2.0 - d1s * r1)
            slope = es * r1
            pivots = jnp.where(odd, d2s - es * slope, d1s)
            scale = inverse_root(pivots)
            def finish(x):
                up = jnp.concatenate([x[:1], x[:-1]], axis=0)
                return (x - slope * up) * scale
            work[t] = finish(work[t])
            unit[t] = finish(unit[t])
        if last < count:
            rows = jnp.concatenate(work[per * b : last], axis=0)
            both = jnp.concatenate([rows, jnp.concatenate(unit[per * b : last], axis=0)], axis=1)
            rh, rl = split(rows)
            bh, bl = split(both)
            left = jnp.concatenate([rh, rh, rl], axis=0)
            right = jnp.concatenate([bh, bl, bh], axis=0)
            update = dot(left, right, ((0,), (0,)))
            for i in range(last, count):
                work[i] = work[i] - update[SUB * i : SUB * (i + 1), :n]
                unit[i] = unit[i] - update[SUB * i : SUB * (i + 1), n:]
        hook()
    return jnp.concatenate(unit, axis=0)


def kernel(rows_count, cols_count, panel, slab, factor_out, schur_out,
           lead, rows, far, slab_in, local_sem, low_h, low_l, own_h, own_l, far_h, far_l,
           lead_recv, rows_recv, far_recv, lead_down, lead_cross, lead_sib, lead_par,
           rows_sib, rows_par, far_up, far_down, far_cross):
    r, c = lax.axis_index("row"), lax.axis_index("col")
    size, width = panel.shape
    chunks = cols_count
    step = size // chunks
    core = c % 2
    sibling = c + 1 - 2 * core
    partner = r + 1 - 2 * (r % 2)
    pairs = cols_count // 2
    root = 1 + c % (rows_count - 1)
    on_chain = (root % 2) == (r % 2)

    def to(row, col):
        return {"row": row, "col": col}

    def peer(i):
        return 2 * ((c // 2 + i + 1) % pairs) + core

    barrier = pltpu.get_barrier_semaphore()

    def greet(row, col):
        pl.semaphore_signal(barrier, inc=1, device_id=to(row, col), device_id_type=pl.DeviceIdType.MESH)

    greet(r, sibling)
    for i in range(pairs - 1):
        greet(r, peer(i))
    greet(partner, c)
    has_up, has_down = r >= 2, r + 2 < rows_count

    @pl.when(has_up)
    def _():
        greet(r - 2, c)

    @pl.when(has_down)
    def _():
        greet(r + 2, c)

    panel_copy = pltpu.make_async_copy(panel, rows.at[c], local_sem.at[0])
    lead_own = pltpu.make_async_copy(panel, lead.at[c], local_sem.at[1])
    slab_copy = pltpu.make_async_copy(slab, slab_in, local_sem.at[2])

    @pl.when(r == 0)
    def _():
        lead_own.start()

    panel_copy.start()
    slab_copy.start()
    pl.semaphore_wait(barrier, 1 + pairs + has_up.astype(jnp.int32) + has_down.astype(jnp.int32))

    def copy(src, dst, send, recv, row, col):
        return pltpu.make_async_remote_copy(src_ref=src, dst_ref=dst, send_sem=send, recv_sem=recv,
                                            device_id=to(row, col), device_id_type=pl.DeviceIdType.MESH)

    def lead_copy(block, q, send, row, col):
        part = lead.at[block, pl.ds(q * step, step), :]
        return copy(part, part, send, lead_recv.at[block, q], row, col)

    def rows_copy(block, send, col):
        return copy(rows.at[block], rows.at[block], send, rows_recv.at[block], r, col)

    def far_copy(block, send, row):
        return copy(far.at[block], far.at[block], send, far_recv.at[block], row, c)

    def lead_arrived(block, q):
        lead_copy(block, q, lead_down.at[0], r, sibling).wait_recv()

    def rows_arrived(block):
        rows_copy(block, rows_par.at[0], sibling).wait_recv()

    def far_arrived(block):
        far_copy(block, far_up.at[0], partner).wait_recv()

    @pl.when(r == 0)
    def _():
        lead_own.wait()

    for q in range(chunks):
        @pl.when(c <= q)
        def _():
            @pl.when(r > 0)
            def _():
                lead_arrived(c, q)

            @pl.when(has_down)
            def _():
                lead_copy(c, q, lead_down.at[q], r + 2, c).start()

            @pl.when(r == 0)
            def _():
                lead_copy(c, q, lead_cross.at[q], 1, c).start()

            for i in range(pairs - 1):
                lead_copy(c, q, lead_par.at[i, q], r, peer(i)).start()
            lead_copy(c, q, lead_sib.at[0, q], r, sibling).start()
    panel_copy.wait()
    for i in range(pairs - 1):
        rows_copy(c, rows_par.at[i], peer(i)).start()
    rows_copy(c, rows_sib.at[0], sibling).start()

    def pass_on(first):
        for i in range(pairs - 1):
            for q in range(chunks):
                @pl.when(((peer(i) == 0) == first) & (peer(i) <= q))
                def _():
                    lead_arrived(peer(i), q)
                    lead_copy(peer(i), q, lead_sib.at[i + 1, q], r, sibling).start()

    pass_on(True)

    reach = (rows_count + 1) // 2
    distance = jnp.abs(root - r) // 2
    hooks = cols_count + reach
    state = {"point": 0, "next": 0}

    def forward(m):
        q = m - distance

        @pl.when(on_chain & (q >= 0) & (q < cols_count))
        def _():
            @pl.when(r == root)
            def _():
                @pl.when(q % 2 != core)
                def _():
                    rows_arrived(q)

                far[q] = rows[q]

            @pl.when(r != root)
            def _():
                far_arrived(q)

            @pl.when((r <= root) & has_up)
            def _():
                far_copy(q, far_up.at[q], r - 2).start()

            @pl.when((r >= root) & has_down)
            def _():
                far_copy(q, far_down.at[q], r + 2).start()

            far_copy(q, far_cross.at[q], partner).start()

    points = width // MID

    def hook(k):
        state["point"] += 1
        if k and state["point"] % points == 1:
            own_rows_ready(k - 1)
        if k and state["point"] % points == 2:
            own_rows(k - 1)
        if state["point"] == 1:
            pass_on(False)
        elif state["point"] == 2:
            for i in range(pairs - 1):
                rows_arrived(peer(i))
                rows_copy(peer(i), rows_sib.at[i + 1], sibling).start()
        elif state["point"] % 2 == 1 and state["next"] < hooks:
            forward(state["next"])
            state["next"] += 1

    lane_ids = lax.broadcasted_iota(jnp.int32, (size, width), 1)
    row_ids = lax.broadcasted_iota(jnp.int32, (size, width), 0)

    def solve(block, k, source, high, low, inverse, top):
        done = k * width
        value = source[k, top:, :]
        if k:
            value = value - dot3((high[top:, :done], low[top:, :done]),
                                 (low_h[done : done + width, :done], low_l[done : done + width, :done]))
        return dot3(split(value), inverse)

    def keep(x, k, high, low, top):
        xh, xl = split(x)
        high[top:, k * width : (k + 1) * width] = xh
        low[top:, k * width : (k + 1) * width] = xl

    def own_rows_ready(k):
        @pl.when((r != root) & (k % 2 != core))
        def _():
            rows_arrived(k)

    def own_rows(k):
        x = solve(None, k, rows, own_h, own_l, inverses[k], 0)
        x = jnp.where(k * width + lane_ids <= r * size + row_ids, x, 0.0)
        keep(x, k, own_h, own_l, 0)

        @pl.when(c == k)
        def _():
            factor_out[...] = x

    inverses = []
    for k in range(cols_count):
        @pl.when(k % 2 != core)
        def _():
            for q in range(k, chunks):
                lead_arrived(k, q)

        first, end = k * width, (k + 1) * width
        square = lead[k, first:end, :]
        if k:
            square = square - dot3((low_h[first:end, :first], low_l[first:end, :first]),
                                   (low_h[first:end, :first], low_l[first:end, :first]))
        inverse = split(lower_inverse(square, functools.partial(hook, k)))
        inverses.append(inverse)
        if k + 1 < cols_count:
            keep(solve(None, k, lead, low_h, low_l, inverse, end), k, low_h, low_l, end)

    own_rows_ready(cols_count - 1)
    own_rows(cols_count - 1)
    if state["next"] < hooks:
        def rest(m, carry):
            forward(m)
            return carry

        lax.fori_loop(state["next"], hooks, rest, 0)
    for k in range(cols_count):
        @pl.when(jnp.logical_not(on_chain))
        def _():
            far_arrived(k)

        x = solve(None, k, far, far_h, far_l, inverses[k], 0)
        x = jnp.where(k * width + lane_ids <= root * size + row_ids, x, 0.0)
        keep(x, k, far_h, far_l, 0)
    slab_copy.wait()
    schur_out[...] = slab_in[...] - dot3((own_h[...], own_l[...]), (far_h[...], far_l[...]))

    for q in range(chunks):
        @pl.when(c <= q)
        def _():
            @pl.when(has_down)
            def _():
                lead_copy(c, q, lead_down.at[q], r + 2, c).wait_send()

            @pl.when(r == 0)
            def _():
                lead_copy(c, q, lead_cross.at[q], 1, c).wait_send()

            for i in range(pairs - 1):
                lead_copy(c, q, lead_par.at[i, q], r, peer(i)).wait_send()
            lead_copy(c, q, lead_sib.at[0, q], r, sibling).wait_send()

        for i in range(pairs - 1):
            @pl.when(peer(i) <= q)
            def _():
                lead_copy(peer(i), q, lead_sib.at[i + 1, q], r, sibling).wait_send()
    rows_copy(c, rows_sib.at[0], sibling).wait_send()
    for i in range(pairs - 1):
        rows_copy(c, rows_par.at[i], peer(i)).wait_send()
        rows_copy(peer(i), rows_sib.at[i + 1], sibling).wait_send()

    @pl.when(on_chain)
    def _():
        for q in range(cols_count):
            @pl.when((r <= root) & has_up)
            def _():
                far_copy(q, far_up.at[q], r - 2).wait_send()

            @pl.when((r >= root) & has_down)
            def _():
                far_copy(q, far_down.at[q], r + 2).wait_send()

            far_copy(q, far_cross.at[q], partner).wait_send()


def shards(rows_count, cols_count, panel, slab):
    size, width = panel.shape
    whole = cols_count * width
    pairs = cols_count // 2
    dma = pltpu.SemaphoreType.DMA
    block = pltpu.VMEM((cols_count, size, width), F32)
    half = pltpu.VMEM((size, whole), BF16)
    vmem, hbm = pl.BlockSpec(memory_space=pltpu.VMEM), pl.BlockSpec(memory_space=pltpu.HBM)
    return pl.pallas_call(
        functools.partial(kernel, rows_count, cols_count),
        out_shape=(jax.ShapeDtypeStruct(panel.shape, F32), jax.ShapeDtypeStruct(slab.shape, F32)),
        in_specs=[hbm, hbm],
        out_specs=(vmem, vmem),
        scratch_shapes=[
            block, block, block, pltpu.VMEM(slab.shape, F32), dma((3,)), half, half, half, half, half, half,
            dma((cols_count, cols_count)), dma((cols_count,)), dma((cols_count,)),
            dma((cols_count,)), dma((cols_count,)), dma((pairs, cols_count)), dma((pairs, cols_count)),
            dma((pairs,)), dma((pairs,)),
            dma((cols_count,)), dma((cols_count,)), dma((cols_count,)),
        ],
        compiler_params=pltpu.CompilerParams(
            collective_id=0, has_side_effects=True, vmem_limit_bytes=63 * 1024 * 1024
        ),
    )(panel, slab)


def solution(mesh):
    placed = (P("row", "col"), P("row", "col"))
    return jax.shard_map(
        functools.partial(shards, mesh.shape["row"], mesh.shape["col"]),
        mesh=mesh,
        in_specs=placed,
        out_specs=placed,
        check_vma=False,
    )
```

```python
import functools

import jax
import jax.numpy as jnp
from jax import lax
from jax.experimental import pallas as pl
from jax.experimental.pallas import tpu as pltpu
from jax.sharding import PartitionSpec as P

F32, BF16 = jnp.float32, jnp.bfloat16
SUB = 8
MID = 32


def split(x):
    high = x.astype(BF16)
    return high, (x - high.astype(F32)).astype(BF16)


def dot(a, b, dims):
    return lax.dot_general(a, b, (dims, ((), ())), preferred_element_type=F32)


def dot3(a, b, dims=((1,), (1,))):
    (ah, al), (bh, bl) = a, b
    return dot(ah, bh, dims) + (dot(ah, bl, dims) + dot(al, bh, dims))


def sublane(x, j):
    return jnp.broadcast_to(x[j : j + 1, :], x.shape)


def lane(x, j):
    return jnp.broadcast_to(x[:, j : j + 1], x.shape)


def inverse_root(p):
    s = lax.rsqrt(p)
    return s * (1.5 - 0.5 * p * s * s)


def lower_inverse(square, hook):
    n = square.shape[0]
    count = n // SUB
    row_ids = lax.broadcasted_iota(jnp.int32, (SUB, n), 0)
    lane_ids = lax.broadcasted_iota(jnp.int32, (SUB, n), 1)
    work = [square[SUB * i : SUB * (i + 1)] for i in range(count)]
    unit = [jnp.where(lane_ids == row_ids + SUB * i, 1.0, 0.0).astype(F32) for i in range(count)]
    per = MID // SUB
    for b in range(n // MID):
        last = per * (b + 1)
        for t in range(per * b, last):
            cols = {i: [lane(work[i], SUB * t + j) for j in range(SUB)] for i in range(t, last)}
            d1s = jnp.ones((SUB, n), F32); d2s = d1s; es = jnp.zeros((SUB, n), F32)
            for j in range(0, SUB, 2):
                top, nxt = cols[t][j], cols[t][j + 1]
                d1, e, d2 = sublane(top, j), sublane(nxt, j), sublane(nxt, j + 1)
                det = d1 * d2 - e * e
                inv = pl.reciprocal(det, approx=True)
                first, second = row_ids == j, row_ids == j + 1
                d1s = jnp.where(first | second, d1, d1s)
                es = jnp.where(second, e, es)
                d2s = jnp.where(second, d2, d2s)
                def mixed(x):
                    h1, h2 = sublane(x, j), sublane(x, j + 1)
                    return h1 * d2 - h2 * e, h2 * d1 - h1 * e
                heads = {k: mixed(cols[t][k]) for k in range(j + 2, SUB)}
                wg, ug = mixed(work[t]), mixed(unit[t])
                for i in range(t, last):
                    c1, c2 = cols[i][j], cols[i][j + 1]
                    if i == t:
                        below = row_ids > j + 1
                        c1, c2 = jnp.where(below, c1, 0.0), jnp.where(below, c2, 0.0)
                    for k in range(j + 2, SUB):
                        g1, g2 = heads[k]
                        cols[i][k] = cols[i][k] - (c1 * g1 + c2 * g2) * inv
                    work[i] = work[i] - (c1 * wg[0] + c2 * wg[1]) * inv
                    unit[i] = unit[i] - (c1 * ug[0] + c2 * ug[1]) * inv
            odd = row_ids % 2 == 1
            r1 = pl.reciprocal(d1s, approx=True)
            r1 = r1 * (2.0 - d1s * r1)
            slope = es * r1
            pivots = jnp.where(odd, d2s - es * slope, d1s)
            scale = inverse_root(pivots)
            def finish(x):
                up = jnp.concatenate([x[:1], x[:-1]], axis=0)
                return (x - slope * up) * scale
            work[t] = finish(work[t])
            unit[t] = finish(unit[t])
        if last < count:
            rows = jnp.concatenate(work[per * b : last], axis=0)
            both = jnp.concatenate([rows, jnp.concatenate(unit[per * b : last], axis=0)], axis=1)
            rh, rl = split(rows)
            bh, bl = split(both)
            left = jnp.concatenate([rh, rh, rl], axis=0)
            right = jnp.concatenate([bh, bl, bh], axis=0)
            update = dot(left, right, ((0,), (0,)))
            for i in range(last, count):
                work[i] = work[i] - update[SUB * i : SUB * (i + 1), :n]
                unit[i] = unit[i] - update[SUB * i : SUB * (i + 1), n:]
        hook()
    return jnp.concatenate(unit, axis=0)


def kernel(rows_count, cols_count, panel, slab, factor_out, schur_out,
           lead, rows, far, slab_in, local_sem, low_h, low_l, own_h, own_l, far_h, far_l,
           lead_recv, rows_recv, far_recv, lead_down, lead_cross, lead_sib, lead_par,
           rows_sib, rows_par, far_up, far_down, far_cross):
    r, c = lax.axis_index("row"), lax.axis_index("col")
    size, width = panel.shape
    chunks = cols_count
    step = size // chunks
    core = c % 2
    sibling = c + 1 - 2 * core
    partner = r + 1 - 2 * (r % 2)
    pairs = cols_count // 2
    root = 1 + c % (rows_count - 1)
    on_chain = (root % 2) == (r % 2)

    def to(row, col):
        return {"row": row, "col": col}

    def peer(i):
        return 2 * ((c // 2 + i + 1) % pairs) + core

    barrier = pltpu.get_barrier_semaphore()

    def greet(row, col):
        pl.semaphore_signal(barrier, inc=1, device_id=to(row, col), device_id_type=pl.DeviceIdType.MESH)

    greet(r, sibling)
    for i in range(pairs - 1):
        greet(r, peer(i))
    greet(partner, c)
    has_up, has_down = r >= 2, r + 2 < rows_count

    @pl.when(has_up)
    def _():
        greet(r - 2, c)

    @pl.when(has_down)
    def _():
        greet(r + 2, c)

    panel_copy = pltpu.make_async_copy(panel, rows.at[c], local_sem.at[0])
    lead_own = pltpu.make_async_copy(panel, lead.at[c], local_sem.at[1])
    slab_copy = pltpu.make_async_copy(slab, slab_in, local_sem.at[2])

    @pl.when(r == 0)
    def _():
        lead_own.start()

    panel_copy.start()
    slab_copy.start()
    pl.semaphore_wait(barrier, 1 + pairs + has_up.astype(jnp.int32) + has_down.astype(jnp.int32))

    def copy(src, dst, send, recv, row, col):
        return pltpu.make_async_remote_copy(src_ref=src, dst_ref=dst, send_sem=send, recv_sem=recv,
                                            device_id=to(row, col), device_id_type=pl.DeviceIdType.MESH)

    def lead_copy(block, q, send, row, col):
        part = lead.at[block, pl.ds(q * step, step), :]
        return copy(part, part, send, lead_recv.at[block, q], row, col)

    def rows_copy(block, send, col):
        return copy(rows.at[block], rows.at[block], send, rows_recv.at[block], r, col)

    def far_copy(block, send, row):
        return copy(far.at[block], far.at[block], send, far_recv.at[block], row, c)

    def lead_arrived(block, q):
        lead_copy(block, q, lead_down.at[0], r, sibling).wait_recv()

    def rows_arrived(block):
        rows_copy(block, rows_par.at[0], sibling).wait_recv()

    def far_arrived(block):
        far_copy(block, far_up.at[0], partner).wait_recv()

    @pl.when(r == 0)
    def _():
        lead_own.wait()

    panel_copy.wait()

    def send_rows():
        for i in range(pairs - 1):
            rows_copy(c, rows_par.at[i], peer(i)).start()
        rows_copy(c, rows_sib.at[0], sibling).start()

    def pass_rows():
        for i in range(pairs - 1):
            rows_arrived(peer(i))
            rows_copy(peer(i), rows_sib.at[i + 1], sibling).start()

    @pl.when(r > 0)
    def _():
        send_rows()

    for q in range(chunks):
        @pl.when(c <= q)
        def _():
            @pl.when(r > 0)
            def _():
                lead_arrived(c, q)

            @pl.when(has_down)
            def _():
                lead_copy(c, q, lead_down.at[q], r + 2, c).start()

            @pl.when(r == 0)
            def _():
                lead_copy(c, q, lead_cross.at[q], 1, c).start()

            for i in range(pairs - 1):
                lead_copy(c, q, lead_par.at[i, q], r, peer(i)).start()
            lead_copy(c, q, lead_sib.at[0, q], r, sibling).start()
    @pl.when(r == 0)
    def _():
        send_rows()

    def pass_on(first):
        for i in range(pairs - 1):
            for q in range(chunks):
                @pl.when(((peer(i) == 0) == first) & (peer(i) <= q))
                def _():
                    lead_arrived(peer(i), q)
                    lead_copy(peer(i), q, lead_sib.at[i + 1, q], r, sibling).start()

    pass_on(True)

    reach = (rows_count + 1) // 2
    distance = jnp.abs(root - r) // 2
    hooks = cols_count + reach

    def turn(o):
        return 2 * ((c // 2 + o // 2) % pairs) + (core + o) % 2

    def far_send(q):
        @pl.when((r <= root) & has_up)
        def _():
            far_copy(q, far_up.at[q], r - 2).start()

        @pl.when((r >= root) & has_down)
        def _():
            far_copy(q, far_down.at[q], r + 2).start()

        far_copy(q, far_cross.at[q], partner).start()

    state = {"point": 0, "next": 0}

    def forward(m):
        o = m + 1 - distance

        @pl.when(on_chain & (r != root) & (o >= 0) & (o < cols_count))
        def _():
            far_arrived(turn(o))
            far_send(turn(o))

    @pl.when(r > 0)
    def _():
        pass_rows()

    @pl.when(r == root)
    def _():
        for o in range(cols_count):
            q = turn(o)
            if o % 2:
                rows_arrived(q)
            far[q] = rows[q]
            far_send(q)

    points = width // MID

    def hook(k):
        state["point"] += 1
        if k and state["point"] % points == 1:
            own_rows_ready(k - 1)
        if k and state["point"] % points == 2:
            own_rows(k - 1)
        if state["point"] == 1:
            pass_on(False)
        elif state["point"] == 2:
            @pl.when(r == 0)
            def _():
                pass_rows()
        elif state["point"] % 2 == 1 and state["next"] < hooks:
            forward(state["next"])
            state["next"] += 1

    lane_ids = lax.broadcasted_iota(jnp.int32, (size, width), 1)
    row_ids = lax.broadcasted_iota(jnp.int32, (size, width), 0)

    def solve(block, k, source, high, low, inverse, top):
        done = k * width
        value = source[k, top:, :]
        if k:
            value = value - dot3((high[top:, :done], low[top:, :done]),
                                 (low_h[done : done + width, :done], low_l[done : done + width, :done]))
        return dot3(split(value), inverse)

    def keep(x, k, high, low, top):
        xh, xl = split(x)
        high[top:, k * width : (k + 1) * width] = xh
        low[top:, k * width : (k + 1) * width] = xl

    def own_rows_ready(k):
        @pl.when((r != root) & (k % 2 != core))
        def _():
            rows_arrived(k)

    def own_rows(k):
        x = solve(None, k, rows, own_h, own_l, inverses[k], 0)
        x = jnp.where(k * width + lane_ids <= r * size + row_ids, x, 0.0)
        keep(x, k, own_h, own_l, 0)

        @pl.when(c == k)
        def _():
            factor_out[...] = x

    inverses = []
    for k in range(cols_count):
        @pl.when(k % 2 != core)
        def _():
            for q in range(k, chunks):
                lead_arrived(k, q)

        first, end = k * width, (k + 1) * width
        square = lead[k, first:end, :]
        if k:
            square = square - dot3((low_h[first:end, :first], low_l[first:end, :first]),
                                   (low_h[first:end, :first], low_l[first:end, :first]))
        inverse = split(lower_inverse(square, functools.partial(hook, k)))
        inverses.append(inverse)
        if k + 1 < cols_count:
            keep(solve(None, k, lead, low_h, low_l, inverse, end), k, low_h, low_l, end)

    own_rows_ready(cols_count - 1)
    own_rows(cols_count - 1)
    if state["next"] < hooks:
        def rest(m, carry):
            forward(m)
            return carry

        lax.fori_loop(state["next"], hooks, rest, 0)
    for k in range(cols_count):
        @pl.when(jnp.logical_not(on_chain))
        def _():
            far_arrived(k)

        x = solve(None, k, far, far_h, far_l, inverses[k], 0)
        x = jnp.where(k * width + lane_ids <= root * size + row_ids, x, 0.0)
        keep(x, k, far_h, far_l, 0)
    slab_copy.wait()
    schur_out[...] = slab_in[...] - dot3((own_h[...], own_l[...]), (far_h[...], far_l[...]))

    for q in range(chunks):
        @pl.when(c <= q)
        def _():
            @pl.when(has_down)
            def _():
                lead_copy(c, q, lead_down.at[q], r + 2, c).wait_send()

            @pl.when(r == 0)
            def _():
                lead_copy(c, q, lead_cross.at[q], 1, c).wait_send()

            for i in range(pairs - 1):
                lead_copy(c, q, lead_par.at[i, q], r, peer(i)).wait_send()
            lead_copy(c, q, lead_sib.at[0, q], r, sibling).wait_send()

        for i in range(pairs - 1):
            @pl.when(peer(i) <= q)
            def _():
                lead_copy(peer(i), q, lead_sib.at[i + 1, q], r, sibling).wait_send()
    rows_copy(c, rows_sib.at[0], sibling).wait_send()
    for i in range(pairs - 1):
        rows_copy(c, rows_par.at[i], peer(i)).wait_send()
        rows_copy(peer(i), rows_sib.at[i + 1], sibling).wait_send()

    @pl.when(on_chain)
    def _():
        for q in range(cols_count):
            @pl.when((r <= root) & has_up)
            def _():
                far_copy(q, far_up.at[q], r - 2).wait_send()

            @pl.when((r >= root) & has_down)
            def _():
                far_copy(q, far_down.at[q], r + 2).wait_send()

            far_copy(q, far_cross.at[q], partner).wait_send()


def shards(rows_count, cols_count, panel, slab):
    size, width = panel.shape
    whole = cols_count * width
    pairs = cols_count // 2
    dma = pltpu.SemaphoreType.DMA
    block = pltpu.VMEM((cols_count, size, width), F32)
    half = pltpu.VMEM((size, whole), BF16)
    vmem, hbm = pl.BlockSpec(memory_space=pltpu.VMEM), pl.BlockSpec(memory_space=pltpu.HBM)
    return pl.pallas_call(
        functools.partial(kernel, rows_count, cols_count),
        out_shape=(jax.ShapeDtypeStruct(panel.shape, F32), jax.ShapeDtypeStruct(slab.shape, F32)),
        in_specs=[hbm, hbm],
        out_specs=(vmem, vmem),
        scratch_shapes=[
            block, block, block, pltpu.VMEM(slab.shape, F32), dma((3,)), half, half, half, half, half, half,
            dma((cols_count, cols_count)), dma((cols_count,)), dma((cols_count,)),
            dma((cols_count,)), dma((cols_count,)), dma((pairs, cols_count)), dma((pairs, cols_count)),
            dma((pairs,)), dma((pairs,)),
            dma((cols_count,)), dma((cols_count,)), dma((cols_count,)),
        ],
        compiler_params=pltpu.CompilerParams(
            collective_id=0, has_side_effects=True, vmem_limit_bytes=48 * 1024 * 1024
        ),
    )(panel, slab)


def solution(mesh):
    placed = (P("row", "col"), P("row", "col"))
    return jax.shard_map(
        functools.partial(shards, mesh.shape["row"], mesh.shape["col"]),
        mesh=mesh,
        in_specs=placed,
        out_specs=placed,
        check_vma=False,
    )
```
